32 devices in a mesh: row: 4 (over z), col: 8 (over y, x, core).
Axes of the slice: x: 2, y: 2, z: 4, core: 2. Of those that a mesh axis runs over, the one named last changes fastest.
Arguments:
- tokens: bfloat16 [512, 12288], P('col', 'row'), may hold values from -6 to 6
- up_weight: bfloat16 [12288, 24576], P('row', 'col'), may hold values from -0.109375 to 0.109375
- up_mask: int32 [192, 384], P('row', 'col'), may hold values 0 or 1
- down_weight: bfloat16 [24576, 12288], P('col', 'row'), may hold values from -0.078125 to 0.078125
- down_mask: int32 [384, 192], P('col', 'row'), may hold values 0 or 1
- grad_out: bfloat16 [512, 12288], P('col', 'row'), may hold values from -6 to 6
Outputs:
- out_heads: bfloat16 [96, 512, 128], P('row', 'col')
- grad_tokens: bfloat16 [512, 12288], P('col', 'row')
- grad_up: bfloat16 [12288, 24576], P('row', 'col')
- grad_down: bfloat16 [24576, 12288], P('col', 'row')
The draws below stay inside these ranges and needn't reach their ends.
All inputs are finite; a program needn't handle non-finite values. No bound on the sum of `up_mask` or of `down_mask` on one device may be relied on, other than what follows from the above.
Results may differ from the reference program's by a relative error of at most 0.022.
Values may be sent and summed in bfloat16 or wider, within the bound.
No kernel may reach another device: no remote copies, remote signals or barrier semaphores. Data moves between devices by JAX's collectives and lax.ppermute only.
A program may use at most 320 MiB of HBM per device.

```python
import math
import jax
import jax.numpy as jnp
from jax import lax

D = 12288
FF = 24576
BLOCK = 64
HEAD_DIM = 128
HEADS = 96
TOKENS = 512
N_ROW = 4
N_COL = 8


def with_ends(entries, stream_key, least, largest):
    place = [jax.random.randint(jax.random.fold_in(stream_key, axis), (), 0, length) for axis, length in enumerate(entries.shape)]
    widest = entries.shape.index(max(entries.shape))
    neighbour = place[:widest] + [(place[widest] + 1) % entries.shape[widest]] + place[widest + 1:]
    return entries.at[tuple(place)].set(least).at[tuple(neighbour)].set(largest)


def levels(own_key, extent, pieces, low, top_value):
    loudness = 1.0
    for axis_at, blocks in pieces:
        steps = jax.random.uniform(jax.random.fold_in(jax.random.fold_in(own_key, 6), axis_at), (blocks,), jnp.float32, low / len(pieces), top_value / len(pieces))
        loudness = loudness * jnp.repeat(jnp.exp(steps), extent[axis_at] // blocks).reshape((-1,) + (1,) * (len(extent) - 1 - axis_at))
    return loudness


def centred(rng, dims, spread, reach, pieces=(), kind=jnp.bfloat16):
    loudness = levels(rng, dims, pieces, -0.22, 0.18) if pieces else 1.0
    array = jax.random.normal(rng, dims, jnp.float32) * spread * loudness
    return jnp.minimum(jnp.maximum(array, -reach), reach).astype(kind)


def setup_inputs(seed: int = 0) -> dict:
    splits = jax.random.split(jax.random.key(seed), 7)
    return {
        "tokens": centred(splits[0], (TOKENS, D), 1.0, 6.0, ((0, 8), (1, 4))),
        "up_weight": centred(splits[1], (D, FF), (D // 4) ** -0.5, 0.109375, ((0, 4), (1, 8))),
        "up_mask": with_ends((jax.random.randint(splits[2], (D // BLOCK, FF // BLOCK), 0, 4) < 1).astype(jnp.int32), jax.random.fold_in(splits[2], 1), 0, 1),
        "down_weight": centred(splits[3], (FF, D), (FF // 4) ** -0.5, 0.078125, ((0, 8), (1, 4))),
        "down_mask": with_ends((jax.random.randint(splits[4], (FF // BLOCK, D // BLOCK), 0, 4) < 1).astype(jnp.int32), jax.random.fold_in(splits[4], 1), 0, 1),
        "grad_out": centred(splits[5], (TOKENS, D), 1.0, 6.0, ((0, 8), (1, 4))),
    }


def expand(weight, mask):
    rows_in, cols_in = weight.shape
    tiles = weight.reshape(rows_in // BLOCK, BLOCK, cols_in // BLOCK, BLOCK)
    tiles = tiles * mask.astype(weight.dtype)[:, None, :, None]
    return tiles.reshape(rows_in, cols_in)

def activate(value):
    return jax.nn.gelu(value, approximate=True)

def block_sum(left, right, groups, right_t):
    width = left.shape[1] // groups
    acc = None
    for group in range(groups):
        piece = left[:, group * width:(group + 1) * width]
        if right_t:
            other = right[:, group * width:(group + 1) * width]
            term = lax.dot_general(piece, other, (((1,), (1,)), ((), ())), preferred_element_type=jnp.float32)
        else:
            other = right[group * width:(group + 1) * width, :]
            term = jnp.dot(piece, other, preferred_element_type=jnp.float32)
        term = term.astype(jnp.bfloat16).astype(jnp.float32)
        acc = term if acc is None else acc + term
    return acc

def reference(tokens, up_weight, up_mask, down_weight, down_mask, grad_out):
    w_up = expand(up_weight, up_mask)
    w_down = expand(down_weight, down_mask)
    pre_act = block_sum(tokens, w_up, N_ROW, False)
    hidden = activate(pre_act).astype(jnp.bfloat16)
    output = block_sum(hidden, w_down, N_COL, False).astype(jnp.bfloat16)
    out_heads = output.reshape(TOKENS, HEADS, HEAD_DIM).transpose(1, 0, 2)
    grad_hidden = block_sum(grad_out, w_down, N_ROW, True)
    unused, pull = jax.vjp(activate, pre_act)
    grad_pre = pull(grad_hidden)[0].astype(jnp.bfloat16)
    grad_scale = 1.0 / math.sqrt(TOKENS)
    grad_up = lax.dot_general(tokens, grad_pre, (((0,), (0,)), ((), ())), preferred_element_type=jnp.float32)
    grad_up = expand(grad_up * grad_scale, up_mask).astype(jnp.bfloat16)
    grad_down = lax.dot_general(hidden, grad_out, (((0,), (0,)), ((), ())), preferred_element_type=jnp.float32)
    grad_down = expand(grad_down * grad_scale, down_mask).astype(jnp.bfloat16)
    grad_tokens = block_sum(grad_pre, w_up, N_COL, True).astype(jnp.bfloat16)
    return (out_heads, grad_tokens, grad_up, grad_down)
```

```python
import functools
import math

import jax
import jax.numpy as jnp
from jax import lax
from jax.experimental import pallas as pl
from jax.experimental.pallas import tpu as pltpu
from jax.sharding import PartitionSpec as P

BLOCK = 64
HEAD_DIM = 128
TILE = 512
ROW_STEP = 16
VMEM_LIMIT = 40 * 1024 * 1024
GELU_A = 0.7978845608
GELU_B = 0.044715


def lane_mask(mask_rows, width, first_block):
    blocks = mask_rows.shape[1]
    block = lax.broadcasted_iota(jnp.int32, (blocks, width), 0)
    column = lax.broadcasted_iota(jnp.int32, (blocks, width), 1)
    pick = (column // BLOCK + first_block == block).astype(jnp.float32)
    return jnp.dot(mask_rows.astype(jnp.float32), pick, preferred_element_type=jnp.float32)


def stack_into(scratch, refs):
    at = 0
    for ref in refs:
        scratch[at : at + ref.shape[0], :] = ref[...]
        at += ref.shape[0]


def weight_kernel(n_in, n_out, transposed, x_refs, tail, out_refs, scratch):
    w_ref, mask_ref = tail
    x_all, w_kept = scratch
    step = pl.program_id(0)

    @pl.when(step == 0)
    def _():
        stack_into(x_all, x_refs)

    depth, width = w_ref.shape
    if transposed:
        blocks = depth // BLOCK
        mask_rows = mask_ref[pl.ds(pl.multiple_of(step * blocks, blocks), blocks), :]
        kept = lane_mask(mask_rows, width, 0)
    else:
        kept = lane_mask(mask_ref[...], width, step * (width // BLOCK))
    kept = kept.astype(jnp.bfloat16)
    for block in range(depth // BLOCK):
        rows = slice(block * BLOCK, (block + 1) * BLOCK)
        w_kept[rows, :] = w_ref[rows, :] * kept[block : block + 1, :]
    contract = ((1,), (1,)) if transposed else ((1,), (0,))
    product = lax.dot_general(
        x_all[...], w_kept[...], (contract, ((), ())), preferred_element_type=jnp.float32
    )
    at = 0
    for out_ref in out_refs:
        out_ref[...] = product[at : at + out_ref.shape[0], :].astype(out_ref.dtype)
        at += out_ref.shape[0]


def grad_kernel(n_x, scale, refs, tail, out_refs, scratch):
    x_refs, g_refs = refs[:n_x], refs[n_x:]
    (mask_ref,), (out_ref,), (x_all, g_all) = tail, out_refs, scratch
    step = pl.program_id(0)

    @pl.when(step == 0)
    def _():
        stack_into(g_all, g_refs)

    stack_into(x_all, x_refs)
    depth, width = out_ref.shape
    blocks = depth // BLOCK
    mask_rows = mask_ref[pl.ds(pl.multiple_of(step * blocks, blocks), blocks), :]
    kept = lane_mask(mask_rows, width, 0) * scale
    product = lax.dot_general(
        x_all[...], g_all[...], (((0,), (0,)), ((), ())), preferred_element_type=jnp.float32
    )
    for block in range(blocks):
        rows = slice(block * BLOCK, (block + 1) * BLOCK)
        out_ref[rows, :] = (product[rows, :] * kept[block : block + 1, :]).astype(out_ref.dtype)


def gelu_and_slope(value):
    square = value * value
    tanh = jnp.tanh(GELU_A * (value + GELU_B * (value * square)))
    half = 0.5 * (1.0 + tanh)
    slope = half + 0.5 * value * (1.0 - tanh * tanh) * (GELU_A * (1.0 + (3.0 * GELU_B) * square))
    return value * half, slope


def sum_kernel(finish, n_sum, refs, tail, out_refs, scratch):
    @pl.loop(0, refs[0].shape[0] // ROW_STEP)
    def _(step):
        rows = pl.ds(pl.multiple_of(step * ROW_STEP, ROW_STEP), ROW_STEP)
        width = refs[0].shape[1]
        for first in range(0, width, TILE):
            columns = slice(first, first + TILE)
            values = [ref[rows, columns].astype(jnp.float32) for ref in refs]
            total = values[0]
            for value in values[1:n_sum]:
                total = total + value
            for out_ref, result in zip(out_refs, finish(total, *values[n_sum:])):
                out_ref[rows, columns] = result.astype(out_ref.dtype)


def dispatch(kernel, counts, *refs):
    n_pieces, n_tail, n_pass, n_after, n_out = counts
    refs = refs[1:]
    tail = refs[n_pieces : n_pieces + n_tail]
    outs = refs[n_pieces + n_tail + n_pass + n_after :]
    kernel(refs[:n_pieces], tail, outs[:n_out], outs[n_out + n_pass :])


class Order:
    def __init__(self, place):
        self.place = place
        self.last = None

    def call(self, kernel, grid, pieces, piece_specs, tail, tail_specs, outs, out_specs, scratch, passing):
        after = [] if self.last is None else [self.last]
        operands = list(pieces) + list(tail) + list(passing) + after
        anywhere = pl.BlockSpec(memory_space=pl.ANY)
        first_pass = 1 + len(pieces) + len(tail)
        results = pl.pallas_call(
            functools.partial(
                dispatch, kernel, (len(pieces), len(tail), len(passing), len(after), len(outs))
            ),
            grid_spec=pltpu.PrefetchScalarGridSpec(
                num_scalar_prefetch=1,
                grid=grid,
                in_specs=list(piece_specs) + list(tail_specs) + [anywhere] * (len(passing) + len(after)),
                out_specs=list(out_specs) + [anywhere] * len(passing),
                scratch_shapes=scratch,
            ),
            out_shape=list(outs) + [jax.ShapeDtypeStruct(p.shape, p.dtype) for p in passing],
            input_output_aliases={first_pass + i: len(outs) + i for i in range(len(passing))},
            compiler_params=pltpu.CompilerParams(vmem_limit_bytes=VMEM_LIMIT),
            cost_estimate=pl.CostEstimate(flops=1, bytes_accessed=1, transcendentals=0),
        )(self.place, *operands)
        self.last = results[0]
        return list(results)

    def piece(self, piece, width, column):
        if isinstance(piece, tuple):
            array, k = piece
            rows = array.shape[0] // self.place.shape[0]
            return array, rows, pl.BlockSpec((rows, width), lambda j, place: (place[k], column(j)))
        return piece, piece.shape[0], pl.BlockSpec((piece.shape[0], width), lambda j, place: (0, column(j)))

    def times_weight(self, pieces, weight, mask, splits, transposed, passing=(), tile=TILE):
        depth, width = weight.shape
        x_width, out_width = (width, depth) if transposed else (depth, width)
        arrays, rows, specs = zip(*[self.piece(p, x_width, lambda j: 0) for p in pieces])
        w_block = (tile, width) if transposed else (depth, tile)
        w_map = (lambda j, place: (j, 0)) if transposed else (lambda j, place: (0, j))
        return self.call(
            functools.partial(weight_kernel, len(pieces), len(splits), transposed),
            (out_width // tile,),
            arrays,
            specs,
            [weight, mask],
            [pl.BlockSpec(w_block, w_map), pl.BlockSpec(mask.shape, lambda j, place: (0, 0))],
            [jax.ShapeDtypeStruct((split, out_width), jnp.bfloat16) for split in splits],
            [pl.BlockSpec((split, tile), lambda j, place: (0, j)) for split in splits],
            [pltpu.VMEM((sum(rows), x_width), jnp.bfloat16), pltpu.VMEM(w_block, jnp.bfloat16)],
            passing,
        )

    def weight_grad(self, x_pieces, g_pieces, mask, depth, width, scale, passing=(), tile=TILE):
        x_arrays, x_rows, x_specs = zip(*[self.piece(p, tile, lambda j: j) for p in x_pieces])
        g_arrays, g_rows, g_specs = zip(*[self.piece(p, width, lambda j: 0) for p in g_pieces])
        return self.call(
            functools.partial(grad_kernel, len(x_pieces), scale),
            (depth // tile,),
            x_arrays + g_arrays,
            x_specs + g_specs,
            [mask],
            [pl.BlockSpec(mask.shape, lambda j, place: (0, 0))],
            [jax.ShapeDtypeStruct((depth, width), jnp.bfloat16)],
            [pl.BlockSpec((tile, width), lambda j, place: (j, 0))],
            [pltpu.VMEM((sum(x_rows), tile), jnp.bfloat16), pltpu.VMEM((sum(g_rows), width), jnp.bfloat16)],
            passing,
        )

    def summed(self, finish, arrays, others, n_out, passing=()):
        shape = arrays[0].shape
        whole = pl.BlockSpec(shape, lambda j, place: (0, 0))
        operands = list(arrays) + list(others)
        return self.call(
            functools.partial(sum_kernel, finish, len(arrays)),
            (1,),
            operands,
            [whole] * len(operands),
            [],
            [],
            [jax.ShapeDtypeStruct(shape, jnp.bfloat16)] * n_out,
            [whole] * n_out,
            [],
            passing,
        )


def only_sum(total):
    return (total,)


class Chain:
    def __init__(self, order, n_row):
        self.order, self.n_row, self.got = order, n_row, []

    def send(self, value):
        hop = len(self.got)
        pairs = [(hop, hop + 1), (self.n_row - 1 - hop, self.n_row - 2 - hop)]
        self.got.append(lax.ppermute(value, "row", pairs))

    def start(self, part):
        self.part = part
        self.send(part)

    def advance(self, passing=()):
        total, *passed = self.order.summed(only_sum, [self.part, self.got[-1]], [], 1, passing)
        self.send(total)
        return passed

    def total(self, finish, others, n_out, passing=()):
        return self.order.summed(finish, [self.part] + self.got, others, n_out, passing)


def body(tokens, up_weight, up_mask, down_weight, down_mask, grad_out):
    n_row, n_col = lax.axis_size("row"), lax.axis_size("col")
    share, model = tokens.shape
    hidden_units = up_weight.shape[1]
    grad_scale = 1.0 / math.sqrt(share * n_col)
    chips = n_col // 2
    place = lax.axis_index("col") ^ jnp.arange(n_col, dtype=jnp.int32)
    order = Order(place)

    def swap(value, offset):
        return lax.ppermute(value, "col", [(i, i ^ offset) for i in range(n_col)])

    tok = [tokens, swap(tokens, 1)] + [None] * (n_col - 2)
    cot_partner = swap(grad_out, 1)
    for offset in range(2, n_col, 2):
        tok[offset] = swap(tokens, offset)
    for offset in range(2, n_col, 2):
        tok[offset + 1] = swap(tok[offset], 1)
    cot_all = lax.all_gather(grad_out, "col", axis=0, tiled=True)
    cot = [grad_out, cot_partner] + [(cot_all, k) for k in range(2, n_col)]

    sizes = [share, share] + [2 * share] * (chips - 1)
    n_chunk = len(sizes)
    queue = [("a", 0), ("a", 1), ("b", 1), ("a", 2), ("a", 3), ("b", 2)]
    for chunk in range(4, n_chunk):
        queue += [("a", chunk), ("b", chunk - 1)]
    queue += [("b", n_chunk - 1), ("b", 0)]
    parts, chains = {}, {}
    hidden, slope, grad_pre = {}, {}, {}
    for key in queue:
        chains[key] = Chain(order, n_row)

    def pass_next(kernel, key):
        if key is None:
            return kernel(())
        *results, part = kernel((parts[key],))
        chains[key].start(part)
        return results

    def finish(key, passing=()):
        kind, chunk = key
        if kind == "a":
            hidden[chunk], slope[chunk], *passed = chains[key].total(gelu_and_slope, [], 2, passing)
        else:
            grad_pre[chunk], *passed = chains[key].total(lambda total, rise: (total * rise,), [slope[chunk]], 1, passing)
        return passed

    def pre(chunks, passing=()):
        pieces, splits = [], []
        for chunk in chunks:
            pieces += [tok[chunk]] if chunk < 2 else tok[2 * chunk - 2 : 2 * chunk]
            splits.append(sizes[chunk])
        results = order.times_weight(pieces, up_weight, up_mask, splits, False, passing)
        for chunk, result in zip(chunks, results):
            parts["a", chunk] = result
        return results[len(chunks) :]

    def back(chunks, passing=()):
        pieces, splits = [], []
        for chunk in chunks:
            pieces += [cot[chunk]] if chunk < 2 else cot[2 * chunk - 2 : 2 * chunk]
            splits.append(sizes[chunk])
        results = order.times_weight(pieces, down_weight, down_mask, splits, True, passing)
        for chunk, result in zip(chunks, results):
            parts["b", chunk] = result
        return results[len(chunks) :]

    def up_back(chunks, passing=()):
        splits = []
        for chunk in chunks:
            splits += [share] if chunk < 2 else [share, share]
        return order.times_weight([grad_pre[chunk] for chunk in chunks], up_weight, up_mask, splits, True, passing)

    def pair_sum(keep, give):
        return order.summed(only_sum, [keep, swap(give, 1)], [], 1)[0]

    tok_parts, out_got, tok_got = [None] * n_col, [], []
    results = {}

    def work_out(passing):
        out, *rest = [order.times_weight([hidden[c] for c in range(n_chunk)], down_weight, down_mask, [share] * n_col, False, passing)], ()
        outs = out[0]
        results["out"] = outs[:n_col]
        return outs[n_col:]

    def work_down(passing):
        down, *passed = order.weight_grad(
            [hidden[c] for c in range(n_chunk)], cot, down_mask, hidden_units, model, grad_scale, passing
        )
        results["down"] = down
        return passed

    def work_tok(chunks):
        def run(passing):
            outs = up_back(chunks, passing)
            at = 0
            for chunk in chunks:
                first = chunk if chunk < 2 else 2 * chunk - 2
                count = 1 if chunk < 2 else 2
                tok_parts[first : first + count] = outs[at : at + count]
                at += count
            return outs[at:]

        return run

    total_slots = len(queue) + n_row - 2
    work = {slot: [] for slot in range(total_slots + 1)}
    place_of = {key: i for i, key in enumerate(queue)}
    work[0] = [lambda passing: pre([2, 3], passing)]
    work[2] = [lambda passing: pre(list(range(4, n_chunk)), passing)]
    work[3] = [lambda passing: back(list(range(2, n_chunk)) + [0], passing)]

    def ready(key):
        return place_of[key] + n_row - 2

    last_a = ready(("a", n_chunk - 1))
    work[last_a].append(work_out)
    work[last_a + 1].append(work_down)
    held = []
    for chunk in range(2, n_chunk):
        slot = ready(("b", chunk))
        if slot == last_a + 1:
            held.append(chunk)
        else:
            work[slot].append(work_tok(held + [chunk]))
            held = []

    pre([0])
    chains[queue[0]].start(parts[queue[0]])
    pre([1])
    chains[queue[1]].start(parts[queue[1]])
    back([1])
    chains[queue[2]].start(parts[queue[2]])
    started = 3
    for slot in range(total_slots + 1):
        for hop in range(n_row - 1):
            at = slot - hop
            if 0 <= at < len(queue):
                if hop < n_row - 2:
                    chains[queue[at]].advance()
                else:
                    finish(queue[at])
        todo = work.get(slot, [])
        for index, step in enumerate(todo):
            key = None
            if index == len(todo) - 1 and slot >= 1 and started < len(queue):
                key = queue[started]
                if key not in parts:
                    step(())
                    chains[key].start(parts[key])
                else:
                    pass_next(step, key)
                started += 1
            else:
                step(())
        if not todo and slot >= 1 and started < len(queue):
            key = queue[started]
            chains[key].start(parts[key])
            started += 1

    work_tok([1])(())
    work_tok([0])(())
    up = order.weight_grad(tok, [grad_pre[c] for c in range(n_chunk)], up_mask, model, hidden_units, grad_scale)

    def over_col(parts_of):
        total = parts_of[0].astype(jnp.float32) + swap(parts_of[1], 1).astype(jnp.float32)
        for offset in range(2, n_col, 2):
            give = swap(parts_of[offset + 1], 1).astype(jnp.float32)
            both = (parts_of[offset].astype(jnp.float32) + give).astype(jnp.bfloat16)
            total = total + swap(both, offset).astype(jnp.float32)
        return total.astype(jnp.bfloat16)

    output_rows = over_col(results["out"])
    grad_tokens = over_col(tok_parts)
    out_heads = output_rows.reshape(share, model // HEAD_DIM, HEAD_DIM).transpose(1, 0, 2)
    return (out_heads, grad_tokens, up[0], results["down"])


def solution(mesh):
    return jax.shard_map(
        body,
        mesh=mesh,
        in_specs=(
            P("col", "row"),
            P("row", "col"),
            P("row", "col"),
            P("col", "row"),
            P("col", "row"),
            P("col", "row"),
        ),
        out_specs=(P("row", "col", None), P("col", "row"), P("row", "col"), P("col", "row")),
        check_vma=False,
    )
```

```python
import functools
import math

import jax
import jax.numpy as jnp
from jax import lax
from jax.experimental import pallas as pl
from jax.experimental.pallas import tpu as pltpu
from jax.sharding import PartitionSpec as P

BLOCK = 64
HEAD_DIM = 128
TILE = 512
ROW_STEP = 16
SLOTS = 4
MATMUL_VMEM = 48 * 1024 * 1024
SUM_VMEM = 14 * 1024 * 1024
COST_STEP = 3500000
GELU_A = 0.7978845608
GELU_B = 0.044715


def lane_mask(mask_rows, width, first_block):
    blocks = mask_rows.shape[1]
    block = lax.broadcasted_iota(jnp.int32, (blocks, width), 0)
    column = lax.broadcasted_iota(jnp.int32, (blocks, width), 1)
    pick = (column // BLOCK + first_block == block).astype(jnp.float32)
    return jnp.dot(mask_rows.astype(jnp.float32), pick, preferred_element_type=jnp.float32)


def span(step, size):
    return pl.ds(pl.multiple_of(step * size, size), size)


def piece_copies(pieces, refs, target, sems):
    copies, at = [], 0
    for index, ((_, first, rows), ref) in enumerate(zip(pieces, refs)):
        copies.append(
            pltpu.make_async_copy(ref.at[pl.ds(first, rows), :], target.at[pl.ds(at, rows), :], sems.at[index])
        )
        at += rows
    return copies


def weight_kernel(pieces, transposed, tile, x_refs, tail, out_refs, scratch):
    w_ref, mask_hbm = tail
    x_all, w_in, w_kept, done, mask_ref, w_sems, x_sems, out_sems, mask_sem = scratch
    depth, width = w_kept.shape
    steps = w_ref.shape[0 if transposed else 1] // tile

    def fetch(step, slot):
        source = w_ref.at[span(step, tile), :] if transposed else w_ref.at[:, span(step, tile)]
        return pltpu.make_async_copy(source, w_in.at[slot], w_sems.at[slot])

    def leave(step, slot):
        copies, at = [], 0
        for index, out_ref in enumerate(out_refs):
            source = done.at[slot, pl.ds(at, out_ref.shape[0]), :]
            copies.append(
                pltpu.make_async_copy(source, out_ref.at[:, span(step, tile)], out_sems.at[slot, index])
            )
            at += out_ref.shape[0]
        return copies

    copies = piece_copies(pieces, x_refs, x_all, x_sems)
    copies.append(pltpu.make_async_copy(mask_hbm, mask_ref, mask_sem))
    fetch(0, 0).start()
    for copy in copies:
        copy.start()
    for step in range(1, min(SLOTS, steps)):
        fetch(step, step).start()
    for copy in copies:
        copy.wait()

    def body(step, carry):
        slot = lax.rem(step, SLOTS)
        fetch(step, slot).wait()
        if transposed:
            kept = lane_mask(mask_ref[span(step, tile // BLOCK), :], width, 0)
        else:
            kept = lane_mask(mask_ref[...], width, step * (tile // BLOCK))
        kept = kept.astype(jnp.bfloat16)
        for block in range(depth // BLOCK):
            rows = slice(block * BLOCK, (block + 1) * BLOCK)
            w_kept[rows, :] = w_in[slot, rows, :] * kept[block : block + 1, :]
        contract = ((1,), (1,)) if transposed else ((1,), (0,))
        product = lax.dot_general(
            x_all[...], w_kept[...], (contract, ((), ())), preferred_element_type=jnp.float32
        )

        @pl.when(step + SLOTS < steps)
        def _():
            fetch(step + SLOTS, slot).start()

        out_slot = lax.rem(step, 2)

        @pl.when(step >= 2)
        def _():
            for copy in leave(step - 2, out_slot):
                copy.wait()

        done[out_slot] = product.astype(done.dtype)
        for copy in leave(step, out_slot):
            copy.start()
        return carry

    lax.fori_loop(0, steps, body, 0)
    for step in range(max(0, steps - 2), steps):
        for copy in leave(step, step % 2):
            copy.wait()


def grad_kernel(x_pieces, g_pieces, scale, tile, refs, tail, out_refs, scratch):
    (mask_hbm,), (out_ref,) = tail, out_refs
    x_all, g_all, done, mask_ref, out_sems, sems, mask_sem = scratch
    count = len(x_pieces)
    copies = piece_copies(x_pieces, refs[:count], x_all, sems)
    copies += piece_copies(g_pieces, refs[count:], g_all, sems.at[pl.ds(count, len(g_pieces))])
    copies.append(pltpu.make_async_copy(mask_hbm, mask_ref, mask_sem))
    for copy in copies:
        copy.start()
    for copy in copies:
        copy.wait()
    depth, width = out_ref.shape
    blocks, steps, slots = tile // BLOCK, depth // tile, done.shape[0]

    def leave(step, slot):
        return pltpu.make_async_copy(done.at[slot], out_ref.at[span(step, tile), :], out_sems.at[slot])

    def body(step, carry):
        slot = lax.rem(step, slots)

        @pl.when(step >= slots)
        def _():
            leave(step - slots, slot).wait()

        kept = lane_mask(mask_ref[span(step, blocks), :], width, 0) * scale
        product = lax.dot_general(
            x_all[:, span(step, tile)], g_all[...], (((0,), (0,)), ((), ())), preferred_element_type=jnp.float32
        )
        for block in range(blocks):
            rows = slice(block * BLOCK, (block + 1) * BLOCK)
            done[slot, rows, :] = (product[rows, :] * kept[block : block + 1, :]).astype(done.dtype)
        leave(step, slot).start()
        return carry

    lax.fori_loop(0, steps, body, 0)
    for step in range(max(0, steps - slots), steps):
        leave(step, step % slots).wait()


def gelu_and_slope(value):
    square = value * value
    tanh = jnp.tanh(GELU_A * (value + GELU_B * (value * square)))
    half = 0.5 * (1.0 + tanh)
    slope = half + 0.5 * value * (1.0 - tanh * tanh) * (GELU_A * (1.0 + (3.0 * GELU_B) * square))
    return value * half, slope


def only_sum(total):
    return (total,)


def sum_kernel(finish, n_sum, splits, heads, refs, tail, out_refs, scratch):
    held, done, in_sems, out_sems = scratch
    width = refs[0].shape[1]
    fetches, first_row = [], 0
    for part, rows in enumerate(splits):
        span_from = pl.ds(first_row, rows)
        fetches.append(
            [
                pltpu.make_async_copy(ref.at[span_from, :], held.at[i, span_from, :], in_sems.at[part, i])
                for i, ref in enumerate(refs)
            ]
        )
        for fetch in fetches[-1]:
            fetch.start()
        first_row += rows
    leaves, first_row = [], 0
    for part, rows in enumerate(splits):
        for fetch in fetches[part]:
            fetch.wait()

        @pl.loop(0, rows // ROW_STEP)
        def _(step, first_row=first_row):
            at = pl.ds(pl.multiple_of(first_row + step * ROW_STEP, ROW_STEP), ROW_STEP)
            for first in range(0, width, TILE):
                columns = slice(first, first + TILE)
                values = [held[i, at, columns].astype(jnp.float32) for i in range(len(refs))]
                total = values[0]
                for value in values[1:n_sum]:
                    total = total + value
                for i, result in enumerate(finish(total, *values[n_sum:])):
                    if heads:
                        for lane in range(0, TILE, HEAD_DIM):
                            head = (first + lane) // HEAD_DIM
                            done[i, head, at, :] = result[:, lane : lane + HEAD_DIM].astype(done.dtype)
                    else:
                        done[i, at, columns] = result.astype(done.dtype)

        for i in range(done.shape[0]):
            source = done.at[i] if heads else done.at[i, pl.ds(first_row, rows), :]
            leaves.append(
                pltpu.make_async_copy(source, out_refs[i * len(splits) + part], out_sems.at[part, i])
            )
            leaves[-1].start()
        first_row += rows
    for leave in leaves:
        leave.wait()


def dispatch(kernel, counts, *refs):
    n_arrays, n_tail, n_pass, n_after, n_out = counts
    tail = refs[n_arrays : n_arrays + n_tail]
    outs = refs[n_arrays + n_tail + n_pass + n_after :]
    kernel(refs[:n_arrays], tail, outs[:n_out], outs[n_out + n_pass + 1 :])


class Order:
    def __init__(self):
        self.last = None

    def call(self, kernel, arrays, tail, outs, scratch, passing, vmem, weight=0.0):
        after = [] if self.last is None else [self.last]
        operands = list(arrays) + list(tail) + list(passing) + after
        token = jax.ShapeDtypeStruct((8, HEAD_DIM), jnp.float32)
        n_out, n_pass = len(outs), len(passing)
        first_pass = len(arrays) + len(tail)
        shapes = list(outs) + [jax.ShapeDtypeStruct(p.shape, p.dtype) for p in passing] + [token]
        *results, self.last = pl.pallas_call(
            functools.partial(dispatch, kernel, (len(arrays), len(tail), n_pass, len(after), n_out)),
            in_specs=[pl.BlockSpec(memory_space=pltpu.HBM)] * len(operands),
            out_specs=[pl.BlockSpec(memory_space=pltpu.HBM)] * len(shapes),
            scratch_shapes=scratch,
            out_shape=shapes,
            input_output_aliases={first_pass + i: n_out + i for i in range(n_pass)},
            compiler_params=pltpu.CompilerParams(vmem_limit_bytes=vmem),
            cost_estimate=pl.CostEstimate(flops=1, bytes_accessed=1 + int(weight * COST_STEP), transcendentals=0),
        )(*operands)
        return results

    def stacked(self, arrays):
        width = arrays[0].shape[1]
        pieces = [whole(array) for array in arrays]

        def kernel(refs, tail, out_refs, scratch):
            copies = piece_copies(pieces, refs, out_refs[0], scratch[0])
            for copy in copies:
                copy.start()
            for copy in copies:
                copy.wait()

        shape = (sum(array.shape[0] for array in arrays), width)
        return self.call(
            kernel,
            arrays,
            [],
            [jax.ShapeDtypeStruct(shape, jnp.bfloat16)],
            [pltpu.SemaphoreType.DMA((len(arrays),))],
            (),
            SUM_VMEM,
        )[0]

    def tied(self, arrays):
        return self.call(lambda refs, tail, out_refs, scratch: None, [], [], [], [], arrays, SUM_VMEM)

    def times_weight(self, pieces, weight, mask, splits, transposed, passing=(), tile=TILE):
        depth, width = weight.shape
        x_width, out_width = (width, depth) if transposed else (depth, width)
        rows = sum(piece[2] for piece in pieces)
        w_block = (tile, width) if transposed else (depth, tile)
        return self.call(
            functools.partial(weight_kernel, pieces, transposed, tile),
            [piece[0] for piece in pieces],
            [weight, mask],
            [jax.ShapeDtypeStruct((split, out_width), jnp.bfloat16) for split in splits],
            [
                pltpu.VMEM((rows, x_width), jnp.bfloat16),
                pltpu.VMEM((SLOTS,) + w_block, jnp.bfloat16),
                pltpu.VMEM(w_block, jnp.bfloat16),
                pltpu.VMEM((2, rows, tile), jnp.bfloat16),
                pltpu.VMEM(mask.shape, mask.dtype),
                pltpu.SemaphoreType.DMA((SLOTS,)),
                pltpu.SemaphoreType.DMA((len(pieces),)),
                pltpu.SemaphoreType.DMA((2, len(splits))),
                pltpu.SemaphoreType.DMA,
            ],
            passing,
            MATMUL_VMEM,
            7.0 + 0.02 * max(0, rows - 128),
        )

    def weight_grad(self, x_pieces, g_pieces, mask, scale, passing=(), tile=TILE):
        pieces = list(x_pieces) + list(g_pieces)
        depth, width = x_pieces[0][0].shape[1], g_pieces[0][0].shape[1]
        return self.call(
            functools.partial(grad_kernel, x_pieces, g_pieces, scale, tile),
            [piece[0] for piece in pieces],
            [mask],
            [jax.ShapeDtypeStruct((depth, width), jnp.bfloat16)],
            [
                pltpu.VMEM((sum(piece[2] for piece in x_pieces), depth), jnp.bfloat16),
                pltpu.VMEM((sum(piece[2] for piece in g_pieces), width), jnp.bfloat16),
                pltpu.VMEM((2, tile, width), jnp.bfloat16),
                pltpu.VMEM(mask.shape, mask.dtype),
                pltpu.SemaphoreType.DMA((2,)),
                pltpu.SemaphoreType.DMA((len(pieces),)),
                pltpu.SemaphoreType.DMA,
            ],
            passing,
            MATMUL_VMEM,
            15.0,
        )

    def summed(self, finish, arrays, others=(), n_out=1, splits=None, heads=False, passing=()):
        rows, width = arrays[0].shape
        splits = splits or [rows]
        operands = list(arrays) + list(others)
        shapes = [(width // HEAD_DIM, rows, HEAD_DIM)] if heads else [(split, width) for split in splits]
        whole_shape = shapes[0] if heads else (rows, width)
        outs = [jax.ShapeDtypeStruct(shape, jnp.bfloat16) for shape in shapes] * n_out
        return self.call(
            functools.partial(sum_kernel, finish, len(arrays), splits, heads),
            operands,
            [],
            outs,
            [
                pltpu.VMEM((len(operands), rows, width), jnp.bfloat16),
                pltpu.VMEM((n_out,) + whole_shape, jnp.bfloat16),
                pltpu.SemaphoreType.DMA((len(splits), len(operands))),
                pltpu.SemaphoreType.DMA((len(splits), n_out)),
            ],
            passing,
            SUM_VMEM,
        )


class Chain:
    def __init__(self, order, n_row):
        self.order, self.n_row, self.got = order, n_row, []

    def send(self, value):
        hop = len(self.got)
        pairs = [(hop, hop + 1), (self.n_row - 1 - hop, self.n_row - 2 - hop)]
        self.got.append(lax.ppermute(value, "row", pairs))

    def start(self, part):
        self.part = part
        self.send(part)

    def advance(self):
        self.send(self.order.summed(only_sum, [self.part, self.got[-1]])[0])

    def total(self, finish, others, n_out):
        return self.order.summed(finish, [self.part] + self.got, others, n_out)


def whole(array):
    return (array, 0, array.shape[0])


def halving(n_col):
    places = [0]
    bit = n_col // 2
    while bit:
        places = places + [place + bit for place in places]
        bit //= 2
    return places


def body(tokens, up_weight, up_mask, down_weight, down_mask, grad_out):
    n_row, n_col = lax.axis_size("row"), lax.axis_size("col")
    share = tokens.shape[0]
    grad_scale = 1.0 / math.sqrt(share * n_col)
    chips = n_col // 2
    order = Order()

    def swap(value, offset):
        return lax.ppermute(value, "col", [(i, i ^ offset) for i in range(n_col)])

    tok, cot = [whole(tokens)] + [None] * (n_col - 1), [whole(grad_out)] + [None] * (n_col - 1)
    for offset in range(1, min(6, n_col)):
        tok[offset] = whole(swap(tokens, offset))

    def hold_stacked(offset, value):
        tok[offset], cot[offset] = (value, 0, share), (value, share, share)

    offsets = [[2 * chip, 2 * chip + 1] for chip in range(chips)]
    queue = [("a", c) for c in range(chips)] + [("b", c) for c in range(1, chips)] + [("b", 0)]
    chains = {key: Chain(order, n_row) for key in queue}
    parts, hidden, slope, grad_pre = {}, {}, {}, {}
    results, tok_sums = {}, {}

    def shard_of(held, offset):
        return (held[offset // 2], (offset % 2) * share, share)

    def finish(key):
        kind, chunk = key
        if kind == "a":
            hidden[chunk], slope[chunk] = chains[key].total(gelu_and_slope, [], 2)
        else:
            (grad_pre[chunk],) = chains[key].total(lambda total, rise: (total * rise,), [slope[chunk]], 1)

    def partial(kind, chunks):
        source, weight, mask = (tok, up_weight, up_mask) if kind == "a" else (cot, down_weight, down_mask)

        def run(passing=()):
            pieces = [source[offset] for chunk in chunks for offset in offsets[chunk]]
            outs = order.times_weight(pieces, weight, mask, [2 * share] * len(chunks), kind == "b", passing)
            for chunk, out in zip(chunks, outs):
                parts[kind, chunk] = out
            return outs[len(chunks) :]

        return run

    def work_out(passing=()):
        pieces = [shard_of(hidden, offset) for offset in halving(n_col)]
        half = share * n_col // 2
        results["keep"], results["give"], *passed = order.times_weight(
            pieces, down_weight, down_mask, [half, half], False, passing
        )
        results["bit"] = 1
        return passed

    def give_out():
        (give,) = order.tied([results["give"]])
        results["got"] = swap(give, results["bit"])

    def halve_out(passing=()):
        rows = results["keep"].shape[0]
        arrays = [results["keep"], results["got"]]
        if rows == share:
            results["out"], *passed = order.summed(only_sum, arrays, heads=True, passing=passing)
            return passed
        results["keep"], results["give"], *passed = order.summed(
            only_sum, arrays, splits=[rows // 2, rows // 2], passing=passing
        )
        results["bit"] *= 2
        return passed

    def work_down(passing=()):
        results["down"], *passed = order.weight_grad(
            [whole(hidden[c]) for c in range(chips)],
            [cot[offset] for chunk in offsets for offset in chunk],
            down_mask,
            grad_scale,
            passing,
        )
        return passed

    pending = []

    def work_tok(chunks):
        def run(passing=()):
            kept = [offset for chunk in chunks for offset in offsets[chunk] if offset % 2 == 0]
            given = [offset for chunk in chunks for offset in offsets[chunk] if offset % 2]
            pieces = [shard_of(grad_pre, offset) for offset in kept + given]
            splits = [share * len(group) for group in (kept, given) if group]
            outs = order.times_weight(pieces, up_weight, up_mask, splits, True, passing)
            if chunks == [0]:
                tok_sums[0], tok_sums[1] = outs[0], swap(outs[1], 1)
            else:
                pending.append((kept, outs[0], swap(outs[1], 1)))
            return outs[len(splits) :]

        return run

    def pair_sums():
        while pending:
            kept, keep, got = pending.pop(0)
            sums = order.summed(only_sum, [keep, got], splits=[share] * len(kept))
            for offset, value in zip(kept, sums):
                tok_sums[offset] = swap(value, offset)

    last_slot = len(queue) + n_row - 3
    place_of = {key: i for i, key in enumerate(queue)}

    def ready(key):
        return place_of[key] + n_row - 2

    work = {slot: [] for slot in range(last_slot + 1)}
    work[1].append(partial("a", list(range(3, chips))))
    work[2].append(partial("b", list(range(1, chips)) + [0]))
    last_a = ready(("a", chips - 1))
    work[last_a].append(work_out)
    work[last_a + 1].append(work_down)
    held = []
    for chunk in range(1, chips):
        held.append(chunk)
        if ready(("b", chunk)) > last_a + 1:
            work[ready(("b", chunk))].append(work_tok(held))
            held = []

    started = 1

    def start_next(step):
        nonlocal started
        key = queue[started] if started < len(queue) else None
        passing = (parts[key],) if key in parts else ()
        passed = step(passing) if step else order.tied(passing) if passing else ()
        if key is not None:
            parts[key] = passed[0] if passing else parts[key]
            chains[key].start(parts[key])
            started += 1

    partial("a", [0])()
    chains[queue[0]].start(parts[queue[0]])
    start_next(partial("a", list(range(1, min(3, chips)))))
    both = order.stacked([tokens, grad_out])
    late_cot = order.stacked([grad_out])
    near = [(offset, swap(late_cot, offset)) for offset in range(2, min(6, n_col), 2)]
    for slot in range(last_slot + 1):
        for hop in range(n_row - 1):
            at = slot - hop
            if 0 <= at < len(queue):
                if hop < n_row - 2:
                    chains[queue[at]].advance()
                else:
                    finish(queue[at])
        if slot == 0:
            values = order.tied([value for _, value in near])
            for (offset, _), value in zip(near, values):
                cot[offset], cot[offset + 1] = whole(value), whole(swap(value, 1))
            (both,) = order.tied([both])
            far = [(offset, swap(both, offset)) for offset in range(6, n_col, 2)]
        if slot == 1:
            values = order.tied([value for _, value in far] + [late_cot])
            for (offset, _), value in zip(far, values):
                hold_stacked(offset, value)
                hold_stacked(offset + 1, swap(value, 1))
            cot[1] = whole(swap(values[-1], 1))
        pair_sums()
        steps = list(work[slot])
        if slot > last_a and "out" not in results:
            give_out()
            steps.append(halve_out)
        for step in steps[:-1]:
            step()
        start_next(steps[-1] if steps else None)

    work_tok([0])()
    while "out" not in results:
        give_out()
        halve_out()
    (up,) = order.weight_grad(
        [tok[offset] for chunk in offsets for offset in chunk],
        [whole(grad_pre[c]) for c in range(chips)],
        up_mask,
        grad_scale,
    )
    (grad_tokens,) = order.summed(only_sum, [tok_sums[offset] for offset in sorted(tok_sums)])
    return (results["out"], grad_tokens, up, results["down"])


def solution(mesh):
    return jax.shard_map(
        body,
        mesh=mesh,
        in_specs=(
            P("col", "row"),
            P("row", "col"),
            P("row", "col"),
            P("col", "row"),
            P("col", "row"),
            P("col", "row"),
        ),
        out_specs=(P("row", "col", None), P("col", "row"), P("row", "col"), P("col", "row")),
        check_vma=False,
    )
```

```python
import functools
import math

import jax
import jax.numpy as jnp
from jax import lax
from jax.experimental import pallas as pl
from jax.experimental.pallas import tpu as pltpu
from jax.sharding import PartitionSpec as P

BLOCK = 64
HEAD_DIM = 128
TILE = 512
ROW_STEP = 16
SLOTS = 4
MATMUL_VMEM = 36 * 1024 * 1024
SUM_VMEM = 14 * 1024 * 1024
COST_STEP = 3500000
GELU_A = 0.7978845608
GELU_B = 0.044715


def lane_mask(mask_rows, width, first_block):
    blocks = mask_rows.shape[1]
    block = lax.broadcasted_iota(jnp.int32, (blocks, width), 0)
    column = lax.broadcasted_iota(jnp.int32, (blocks, width), 1)
    pick = (column // BLOCK + first_block == block).astype(jnp.float32)
    return jnp.dot(mask_rows.astype(jnp.float32), pick, preferred_element_type=jnp.float32)


def span(step, size):
    return pl.ds(pl.multiple_of(step * size, size), size)


def piece_copies(pieces, refs, target, sems):
    copies, at = [], 0
    for index, ((_, first, rows), ref) in enumerate(zip(pieces, refs)):
        copies.append(
            pltpu.make_async_copy(ref.at[pl.ds(first, rows), :], target.at[pl.ds(at, rows), :], sems.at[index])
        )
        at += rows
    return copies


def weight_kernel(pieces, transposed, tile, x_refs, tail, out_refs, scratch):
    w_ref, mask_hbm = tail
    x_all, w_in, w_kept, done, mask_ref, w_sems, x_sems, out_sems, mask_sem = scratch
    depth, width = w_kept.shape
    steps = w_ref.shape[0 if transposed else 1] // tile

    def fetch(step, slot):
        source = w_ref.at[span(step, tile), :] if transposed else w_ref.at[:, span(step, tile)]
        return pltpu.make_async_copy(source, w_in.at[slot], w_sems.at[slot])

    def leave(step, slot):
        copies, at = [], 0
        for index, out_ref in enumerate(out_refs):
            source = done.at[slot, pl.ds(at, out_ref.shape[0]), :]
            copies.append(
                pltpu.make_async_copy(source, out_ref.at[:, span(step, tile)], out_sems.at[slot, index])
            )
            at += out_ref.shape[0]
        return copies

    copies = piece_copies(pieces, x_refs, x_all, x_sems)
    copies.append(pltpu.make_async_copy(mask_hbm, mask_ref, mask_sem))
    fetch(0, 0).start()
    for copy in copies:
        copy.start()
    for step in range(1, min(SLOTS, steps)):
        fetch(step, step).start()
    for copy in copies:
        copy.wait()

    def body(step, carry):
        slot = lax.rem(step, SLOTS)
        fetch(step, slot).wait()
        if transposed:
            kept = lane_mask(mask_ref[span(step, tile // BLOCK), :], width, 0)
        else:
            kept = lane_mask(mask_ref[...], width, step * (tile // BLOCK))
        kept = kept.astype(jnp.bfloat16)
        for block in range(depth // BLOCK):
            rows = slice(block * BLOCK, (block + 1) * BLOCK)
            w_kept[rows, :] = w_in[slot, rows, :] * kept[block : block + 1, :]
        contract = ((1,), (1,)) if transposed else ((1,), (0,))
        product = lax.dot_general(
            x_all[...], w_kept[...], (contract, ((), ())), preferred_element_type=jnp.float32
        )

        @pl.when(step + SLOTS < steps)
        def _():
            fetch(step + SLOTS, slot).start()

        out_slot = lax.rem(step, 2)

        @pl.when(step >= 2)
        def _():
            for copy in leave(step - 2, out_slot):
                copy.wait()

        done[out_slot] = product.astype(done.dtype)
        for copy in leave(step, out_slot):
            copy.start()
        return carry

    lax.fori_loop(0, steps, body, 0)
    for step in range(max(0, steps - 2), steps):
        for copy in leave(step, step % 2):
            copy.wait()


def grad_kernel(x_pieces, g_pieces, scale, tile, refs, tail, out_refs, scratch):
    (mask_hbm,), (out_ref,) = tail, out_refs
    x_all, g_all, done, mask_ref, out_sems, sems, mask_sem = scratch
    count = len(x_pieces)
    copies = piece_copies(x_pieces, refs[:count], x_all, sems)
    copies += piece_copies(g_pieces, refs[count:], g_all, sems.at[pl.ds(count, len(g_pieces))])
    copies.append(pltpu.make_async_copy(mask_hbm, mask_ref, mask_sem))
    for copy in copies:
        copy.start()
    for copy in copies:
        copy.wait()
    depth, width = out_ref.shape
    blocks, steps, slots = tile // BLOCK, depth // tile, done.shape[0]

    def leave(step, slot):
        return pltpu.make_async_copy(done.at[slot], out_ref.at[span(step, tile), :], out_sems.at[slot])

    def body(step, carry):
        slot = lax.rem(step, slots)

        @pl.when(step >= slots)
        def _():
            leave(step - slots, slot).wait()

        kept = lane_mask(mask_ref[span(step, blocks), :], width, 0) * scale
        product = lax.dot_general(
            x_all[:, span(step, tile)], g_all[...], (((0,), (0,)), ((), ())), preferred_element_type=jnp.float32
        )
        for block in range(blocks):
            rows = slice(block * BLOCK, (block + 1) * BLOCK)
            done[slot, rows, :] = (product[rows, :] * kept[block : block + 1, :]).astype(done.dtype)
        leave(step, slot).start()
        return carry

    lax.fori_loop(0, steps, body, 0)
    for step in range(max(0, steps - slots), steps):
        leave(step, step % slots).wait()


def gelu_and_slope(value):
    square = value * value
    tanh = jnp.tanh(GELU_A * (value + GELU_B * (value * square)))
    half = 0.5 * (1.0 + tanh)
    slope = half + 0.5 * value * (1.0 - tanh * tanh) * (GELU_A * (1.0 + (3.0 * GELU_B) * square))
    return value * half, slope


def only_sum(total):
    return (total,)


def sum_kernel(finish, n_sum, splits, heads, refs, tail, out_refs, scratch):
    held, done, in_sems, out_sems = scratch
    width = refs[0].shape[1]
    fetches, first_row = [], 0
    for part, rows in enumerate(splits):
        span_from = pl.ds(first_row, rows)
        fetches.append(
            [
                pltpu.make_async_copy(ref.at[span_from, :], held.at[i, span_from, :], in_sems.at[part, i])
                for i, ref in enumerate(refs)
            ]
        )
        for fetch in fetches[-1]:
            fetch.start()
        first_row += rows
    leaves, first_row = [], 0
    for part, rows in enumerate(splits):
        for fetch in fetches[part]:
            fetch.wait()

        @pl.loop(0, rows // ROW_STEP)
        def _(step, first_row=first_row):
            at = pl.ds(pl.multiple_of(first_row + step * ROW_STEP, ROW_STEP), ROW_STEP)
            for first in range(0, width, TILE):
                columns = slice(first, first + TILE)
                values = [held[i, at, columns].astype(jnp.float32) for i in range(len(refs))]
                total = values[0]
                for value in values[1:n_sum]:
                    total = total + value
                for i, result in enumerate(finish(total, *values[n_sum:])):
                    if heads:
                        for lane in range(0, TILE, HEAD_DIM):
                            head = (first + lane) // HEAD_DIM
                            done[i, head, at, :] = result[:, lane : lane + HEAD_DIM].astype(done.dtype)
                    else:
                        done[i, at, columns] = result.astype(done.dtype)

        for i in range(done.shape[0]):
            source = done.at[i] if heads else done.at[i, pl.ds(first_row, rows), :]
            leaves.append(
                pltpu.make_async_copy(source, out_refs[i * len(splits) + part], out_sems.at[part, i])
            )
            leaves[-1].start()
        first_row += rows
    for leave in leaves:
        leave.wait()


def dispatch(kernel, counts, *refs):
    n_arrays, n_tail, n_pass, n_after, n_out = counts
    tail = refs[n_arrays : n_arrays + n_tail]
    outs = refs[n_arrays + n_tail + n_pass + n_after :]
    kernel(refs[:n_arrays], tail, outs[:n_out], outs[n_out + n_pass + 1 :])


class Order:
    def __init__(self):
        self.last = None

    def call(self, kernel, arrays, tail, outs, scratch, passing, vmem, weight=0.0):
        after = [] if self.last is None else [self.last]
        operands = list(arrays) + list(tail) + list(passing) + after
        token = jax.ShapeDtypeStruct((8, HEAD_DIM), jnp.float32)
        n_out, n_pass = len(outs), len(passing)
        first_pass = len(arrays) + len(tail)
        shapes = list(outs) + [jax.ShapeDtypeStruct(p.shape, p.dtype) for p in passing] + [token]
        *results, self.last = pl.pallas_call(
            functools.partial(dispatch, kernel, (len(arrays), len(tail), n_pass, len(after), n_out)),
            in_specs=[pl.BlockSpec(memory_space=pltpu.HBM)] * len(operands),
            out_specs=[pl.BlockSpec(memory_space=pltpu.HBM)] * len(shapes),
            scratch_shapes=scratch,
            out_shape=shapes,
            input_output_aliases={first_pass + i: n_out + i for i in range(n_pass)},
            compiler_params=pltpu.CompilerParams(vmem_limit_bytes=vmem),
            cost_estimate=pl.CostEstimate(flops=1, bytes_accessed=1 + int(weight * COST_STEP), transcendentals=0),
        )(*operands)
        return results

    def stacked(self, arrays):
        width = arrays[0].shape[1]
        pieces = [whole(array) for array in arrays]

        def kernel(refs, tail, out_refs, scratch):
            copies = piece_copies(pieces, refs, out_refs[0], scratch[0])
            for copy in copies:
                copy.start()
            for copy in copies:
                copy.wait()

        shape = (sum(array.shape[0] for array in arrays), width)
        return self.call(
            kernel,
            arrays,
            [],
            [jax.ShapeDtypeStruct(shape, jnp.bfloat16)],
            [pltpu.SemaphoreType.DMA((len(arrays),))],
            (),
            SUM_VMEM,
        )[0]

    def tied(self, arrays):
        return self.call(lambda refs, tail, out_refs, scratch: None, [], [], [], [], arrays, SUM_VMEM)

    def times_weight(self, pieces, weight, mask, splits, transposed, passing=(), tile=TILE):
        depth, width = weight.shape
        x_width, out_width = (width, depth) if transposed else (depth, width)
        rows = sum(piece[2] for piece in pieces)
        w_block = (tile, width) if transposed else (depth, tile)
        return self.call(
            functools.partial(weight_kernel, pieces, transposed, tile),
            [piece[0] for piece in pieces],
            [weight, mask],
            [jax.ShapeDtypeStruct((split, out_width), jnp.bfloat16) for split in splits],
            [
                pltpu.VMEM((rows, x_width), jnp.bfloat16),
                pltpu.VMEM((SLOTS,) + w_block, jnp.bfloat16),
                pltpu.VMEM(w_block, jnp.bfloat16),
                pltpu.VMEM((2, rows, tile), jnp.bfloat16),
                pltpu.VMEM(mask.shape, mask.dtype),
                pltpu.SemaphoreType.DMA((SLOTS,)),
                pltpu.SemaphoreType.DMA((len(pieces),)),
                pltpu.SemaphoreType.DMA((2, len(splits))),
                pltpu.SemaphoreType.DMA,
            ],
            passing,
            MATMUL_VMEM,
            7.0 + 0.02 * max(0, rows - 128),
        )

    def weight_grad(self, x_pieces, g_pieces, mask, scale, passing=(), tile=TILE):
        pieces = list(x_pieces) + list(g_pieces)
        depth, width = x_pieces[0][0].shape[1], g_pieces[0][0].shape[1]
        return self.call(
            functools.partial(grad_kernel, x_pieces, g_pieces, scale, tile),
            [piece[0] for piece in pieces],
            [mask],
            [jax.ShapeDtypeStruct((depth, width), jnp.bfloat16)],
            [
                pltpu.VMEM((sum(piece[2] for piece in x_pieces), depth), jnp.bfloat16),
                pltpu.VMEM((sum(piece[2] for piece in g_pieces), width), jnp.bfloat16),
                pltpu.VMEM((2, tile, width), jnp.bfloat16),
                pltpu.VMEM(mask.shape, mask.dtype),
                pltpu.SemaphoreType.DMA((2,)),
                pltpu.SemaphoreType.DMA((len(pieces),)),
                pltpu.SemaphoreType.DMA,
            ],
            passing,
            MATMUL_VMEM,
            15.0,
        )

    def summed(self, finish, arrays, others=(), n_out=1, splits=None, heads=False, passing=()):
        rows, width = arrays[0].shape
        splits = splits or [rows]
        operands = list(arrays) + list(others)
        shapes = [(width // HEAD_DIM, rows, HEAD_DIM)] if heads else [(split, width) for split in splits]
        whole_shape = shapes[0] if heads else (rows, width)
        outs = [jax.ShapeDtypeStruct(shape, jnp.bfloat16) for shape in shapes] * n_out
        return self.call(
            functools.partial(sum_kernel, finish, len(arrays), splits, heads),
            operands,
            [],
            outs,
            [
                pltpu.VMEM((len(operands), rows, width), jnp.bfloat16),
                pltpu.VMEM((n_out,) + whole_shape, jnp.bfloat16),
                pltpu.SemaphoreType.DMA((len(splits), len(operands))),
                pltpu.SemaphoreType.DMA((len(splits), n_out)),
            ],
            passing,
            SUM_VMEM,
        )


class Chain:
    def __init__(self, order, n_row):
        self.order, self.n_row, self.got = order, n_row, []

    def send(self, value):
        hop = len(self.got)
        pairs = [(hop, hop + 1), (self.n_row - 1 - hop, self.n_row - 2 - hop)]
        self.got.append(lax.ppermute(value, "row", pairs))

    def start(self, part):
        self.part = part
        self.send(part)

    def advance(self):
        self.send(self.order.summed(only_sum, [self.part, self.got[-1]])[0])

    def total(self, finish, others, n_out):
        return self.order.summed(finish, [self.part] + self.got, others, n_out)


def whole(array):
    return (array, 0, array.shape[0])


def halving(n_col):
    places = [0]
    bit = n_col // 2
    while bit:
        places = places + [place + bit for place in places]
        bit //= 2
    return places


def body(tokens, up_weight, up_mask, down_weight, down_mask, grad_out):
    n_row, n_col = lax.axis_size("row"), lax.axis_size("col")
    share = tokens.shape[0]
    grad_scale = 1.0 / math.sqrt(share * n_col)
    chips = n_col // 2
    order = Order()

    def swap(value, offset):
        return lax.ppermute(value, "col", [(i, i ^ offset) for i in range(n_col)])

    tok, cot = [whole(tokens)] + [None] * (n_col - 1), [whole(grad_out)] + [None] * (n_col - 1)
    for offset in range(1, min(6, n_col)):
        tok[offset] = whole(swap(tokens, offset))

    def hold_stacked(offset, value):
        tok[offset], cot[offset] = (value, 0, share), (value, share, share)

    offsets = [[2 * chip, 2 * chip + 1] for chip in range(chips)]
    queue = [("a", c) for c in range(chips)] + [("b", c) for c in range(1, chips)] + [("b", 0)]
    chains = {key: Chain(order, n_row) for key in queue}
    parts, hidden, slope, grad_pre = {}, {}, {}, {}
    results, tok_sums = {}, {}

    def shard_of(held, offset):
        return (held[offset // 2], (offset % 2) * share, share)

    def finish(key):
        kind, chunk = key
        if kind == "a":
            hidden[chunk], slope[chunk] = chains[key].total(gelu_and_slope, [], 2)
        else:
            (grad_pre[chunk],) = chains[key].total(lambda total, rise: (total * rise,), [slope[chunk]], 1)

    def partial(kind, chunks):
        source, weight, mask = (tok, up_weight, up_mask) if kind == "a" else (cot, down_weight, down_mask)

        def run(passing=()):
            pieces = [source[offset] for chunk in chunks for offset in offsets[chunk]]
            outs = order.times_weight(pieces, weight, mask, [2 * share] * len(chunks), kind == "b", passing)
            for chunk, out in zip(chunks, outs):
                parts[kind, chunk] = out
            return outs[len(chunks) :]

        return run

    def work_out(chunks):
        def run(passing=()):
            chosen = [offset for offset in halving(n_col) if offset // 2 in chunks]
            half = share * len(chosen) // 2
            pieces = [shard_of(hidden, offset) for offset in chosen]
            keep, give, *passed = order.times_weight(pieces, down_weight, down_mask, [half, half], False, passing)
            results.setdefault("keeps", []).append(keep)
            results.setdefault("gives", []).append(give)
            results["bit"] = 1
            return passed

        return run

    def give_out():
        if results["bit"] == 1:
            results["keep"], results["give"] = order.stacked(results["keeps"]), order.stacked(results["gives"])
        else:
            (results["give"],) = order.tied([results["give"]])
        results["got"] = swap(results["give"], results["bit"])

    def halve_out(passing=()):
        rows = results["keep"].shape[0]
        arrays = [results["keep"], results["got"]]
        if rows == share:
            results["out"], *passed = order.summed(only_sum, arrays, heads=True, passing=passing)
            return passed
        results["keep"], results["give"], *passed = order.summed(
            only_sum, arrays, splits=[rows // 2, rows // 2], passing=passing
        )
        results["bit"] *= 2
        return passed

    def work_down(passing=()):
        results["down"], *passed = order.weight_grad(
            [whole(hidden[c]) for c in range(chips)],
            [cot[offset] for chunk in offsets for offset in chunk],
            down_mask,
            grad_scale,
            passing,
        )
        return passed

    pending = []

    def work_tok(chunks):
        def run(passing=()):
            kept = [offset for chunk in chunks for offset in offsets[chunk] if offset % 2 == 0]
            given = [offset for chunk in chunks for offset in offsets[chunk] if offset % 2]
            pieces = [shard_of(grad_pre, offset) for offset in kept + given]
            splits = [share * len(group) for group in (kept, given) if group]
            outs = order.times_weight(pieces, up_weight, up_mask, splits, True, passing)
            if chunks == [0]:
                tok_sums[0], tok_sums[1] = outs[0], swap(outs[1], 1)
            else:
                pending.append((kept, outs[0], swap(outs[1], 1)))
            return outs[len(splits) :]

        return run

    def pair_sums():
        while pending:
            kept, keep, got = pending.pop(0)
            sums = order.summed(only_sum, [keep, got], splits=[share] * len(kept))
            for offset, value in zip(kept, sums):
                tok_sums[offset] = swap(value, offset)

    last_slot = len(queue) + n_row - 3
    place_of = {key: i for i, key in enumerate(queue)}

    def ready(key):
        return place_of[key] + n_row - 2

    work = {slot: [] for slot in range(last_slot + 1)}
    work[1].append(partial("a", list(range(3, chips))))
    work[2].append(partial("b", list(range(1, chips)) + [0]))
    last_a = ready(("a", chips - 1))
    work[last_a - 1].append(work_out(list(range(chips - 1))))
    work[last_a].append(work_out([chips - 1]))
    work[last_a + 1].append(work_down)
    held = []
    for chunk in range(1, chips):
        held.append(chunk)
        if ready(("b", chunk)) > last_a + 1:
            work[ready(("b", chunk))].append(work_tok(held))
            held = []

    started = 1

    def start_next(step):
        nonlocal started
        key = queue[started] if started < len(queue) else None
        passing = (parts[key],) if key in parts else ()
        passed = step(passing) if step else order.tied(passing) if passing else ()
        if key is not None:
            parts[key] = passed[0] if passing else parts[key]
            chains[key].start(parts[key])
            started += 1

    partial("a", [0])()
    chains[queue[0]].start(parts[queue[0]])
    start_next(partial("a", list(range(1, min(3, chips)))))
    both = order.stacked([tokens, grad_out])
    late_cot = order.stacked([grad_out])
    near = [(offset, swap(late_cot, offset)) for offset in range(2, min(6, n_col), 2)]
    for slot in range(last_slot + 1):
        for hop in range(n_row - 1):
            at = slot - hop
            if 0 <= at < len(queue):
                if hop < n_row - 2:
                    chains[queue[at]].advance()
                else:
                    finish(queue[at])
        if slot == 0:
            values = order.tied([value for _, value in near])
            for (offset, _), value in zip(near, values):
                cot[offset], cot[offset + 1] = whole(value), whole(swap(value, 1))
            (both,) = order.tied([both])
            far = [(offset, swap(both, offset)) for offset in range(6, n_col, 2)]
        if slot == 1:
            values = order.tied([value for _, value in far] + [late_cot])
            for (offset, _), value in zip(far, values):
                hold_stacked(offset, value)
                hold_stacked(offset + 1, swap(value, 1))
            cot[1] = whole(swap(values[-1], 1))
        pair_sums()
        steps = list(work[slot])
        if slot > last_a and "out" not in results:
            give_out()
            steps.append(halve_out)
        for step in steps[:-1]:
            step()
        start_next(steps[-1] if steps else None)

    work_tok([0])()
    while "out" not in results:
        give_out()
        halve_out()
    (up,) = order.weight_grad(
        [tok[offset] for chunk in offsets for offset in chunk],
        [whole(grad_pre[c]) for c in range(chips)],
        up_mask,
        grad_scale,
    )
    (grad_tokens,) = order.summed(only_sum, [tok_sums[offset] for offset in sorted(tok_sums)])
    return (results["out"], grad_tokens, up, results["down"])


def solution(mesh):
    return jax.shard_map(
        body,
        mesh=mesh,
        in_specs=(
            P("col", "row"),
            P("row", "col"),
            P("row", "col"),
            P("col", "row"),
            P("col", "row"),
            P("col", "row"),
        ),
        out_specs=(P("row", "col", None), P("col", "row"), P("row", "col"), P("col", "row")),
        check_vma=False,
    )
```

```python
import functools
import math

import jax
import jax.numpy as jnp
from jax import lax
from jax.experimental import pallas as pl
from jax.experimental.pallas import tpu as pltpu
from jax.sharding import PartitionSpec as P

BLOCK = 64
HEAD_DIM = 128
TILE = 512
ROW_STEP = 16
SLOTS = 4
MATMUL_VMEM = 36 * 1024 * 1024
SUM_VMEM = 14 * 1024 * 1024
COST_STEP = 3500000
GELU_A = 0.7978845608
GELU_B = 0.044715


def lane_mask(mask_rows, width, first_block):
    blocks = mask_rows.shape[1]
    block = lax.broadcasted_iota(jnp.int32, (blocks, width), 0)
    column = lax.broadcasted_iota(jnp.int32, (blocks, width), 1)
    pick = (column // BLOCK + first_block == block).astype(jnp.float32)
    return jnp.dot(mask_rows.astype(jnp.float32), pick, preferred_element_type=jnp.float32)


def span(step, size):
    return pl.ds(pl.multiple_of(step * size, size), size)


def piece_copies(pieces, refs, target, sems):
    copies, at = [], 0
    for index, ((_, first, rows), ref) in enumerate(zip(pieces, refs)):
        copies.append(
            pltpu.make_async_copy(ref.at[pl.ds(first, rows), :], target.at[pl.ds(at, rows), :], sems.at[index])
        )
        at += rows
    return copies


def weight_kernel(pieces, transposed, tile, x_refs, tail, out_refs, scratch):
    w_ref, mask_hbm = tail
    x_all, w_in, w_kept, done, mask_ref, w_sems, x_sems, out_sems, mask_sem = scratch
    depth, width = w_kept.shape
    steps = w_ref.shape[0 if transposed else 1] // tile

    def fetch(step, slot):
        source = w_ref.at[span(step, tile), :] if transposed else w_ref.at[:, span(step, tile)]
        return pltpu.make_async_copy(source, w_in.at[slot], w_sems.at[slot])

    def leave(step, slot):
        copies, at = [], 0
        for index, out_ref in enumerate(out_refs):
            source = done.at[slot, pl.ds(at, out_ref.shape[0]), :]
            copies.append(
                pltpu.make_async_copy(source, out_ref.at[:, span(step, tile)], out_sems.at[slot, index])
            )
            at += out_ref.shape[0]
        return copies

    copies = piece_copies(pieces, x_refs, x_all, x_sems)
    copies.append(pltpu.make_async_copy(mask_hbm, mask_ref, mask_sem))
    fetch(0, 0).start()
    for copy in copies:
        copy.start()
    for step in range(1, min(SLOTS, steps)):
        fetch(step, step).start()
    for copy in copies:
        copy.wait()

    def body(step, carry):
        slot = lax.rem(step, SLOTS)
        fetch(step, slot).wait()
        if transposed:
            kept = lane_mask(mask_ref[span(step, tile // BLOCK), :], width, 0)
        else:
            kept = lane_mask(mask_ref[...], width, step * (tile // BLOCK))
        kept = kept.astype(jnp.bfloat16)
        for block in range(depth // BLOCK):
            rows = slice(block * BLOCK, (block + 1) * BLOCK)
            w_kept[rows, :] = w_in[slot, rows, :] * kept[block : block + 1, :]
        contract = ((1,), (1,)) if transposed else ((1,), (0,))
        product = lax.dot_general(
            x_all[...], w_kept[...], (contract, ((), ())), preferred_element_type=jnp.float32
        )

        @pl.when(step + SLOTS < steps)
        def _():
            fetch(step + SLOTS, slot).start()

        out_slot = lax.rem(step, 2)

        @pl.when(step >= 2)
        def _():
            for copy in leave(step - 2, out_slot):
                copy.wait()

        done[out_slot] = product.astype(done.dtype)
        for copy in leave(step, out_slot):
            copy.start()
        return carry

    lax.fori_loop(0, steps, body, 0)
    for step in range(max(0, steps - 2), steps):
        for copy in leave(step, step % 2):
            copy.wait()


def grad_kernel(x_pieces, g_pieces, scale, tile, refs, tail, out_refs, scratch):
    (mask_hbm,), (out_ref,) = tail, out_refs
    x_all, x_first, g_all, done, mask_ref, out_sems, sems, first_sems, mask_sem = scratch
    count = len(x_pieces)
    later = piece_copies(x_pieces, refs[:count], x_all, sems)
    columns = [ref.at[:, pl.ds(0, tile)] for ref in refs[:count]]
    copies = piece_copies(x_pieces, columns, x_first, first_sems)
    copies += piece_copies(g_pieces, refs[count:], g_all, sems.at[pl.ds(count, len(g_pieces))])
    copies.append(pltpu.make_async_copy(mask_hbm, mask_ref, mask_sem))
    for copy in copies + later:
        copy.start()
    for copy in copies:
        copy.wait()
    depth, width = out_ref.shape
    blocks, steps, slots = tile // BLOCK, depth // tile, done.shape[0]

    def leave(step, slot):
        return pltpu.make_async_copy(done.at[slot], out_ref.at[span(step, tile), :], out_sems.at[slot])

    def rows_done(step, slot, x_tile):
        kept = lane_mask(mask_ref[span(step, blocks), :], width, 0) * scale
        product = lax.dot_general(
            x_tile, g_all[...], (((0,), (0,)), ((), ())), preferred_element_type=jnp.float32
        )
        for block in range(blocks):
            rows = slice(block * BLOCK, (block + 1) * BLOCK)
            done[slot, rows, :] = (product[rows, :] * kept[block : block + 1, :]).astype(done.dtype)
        leave(step, slot).start()

    def body(step, carry):
        slot = lax.rem(step, slots)

        @pl.when(step >= slots)
        def _():
            leave(step - slots, slot).wait()

        rows_done(step, slot, x_all[:, span(step, tile)])
        return carry

    rows_done(0, 0, x_first[...])
    for copy in later:
        copy.wait()
    lax.fori_loop(1, steps, body, 0)
    for step in range(max(0, steps - slots), steps):
        leave(step, step % slots).wait()


def gelu_and_slope(value):
    square = value * value
    tanh = jnp.tanh(GELU_A * (value + GELU_B * (value * square)))
    half = 0.5 * (1.0 + tanh)
    slope = half + 0.5 * value * (1.0 - tanh * tanh) * (GELU_A * (1.0 + (3.0 * GELU_B) * square))
    return value * half, slope


def only_sum(total):
    return (total,)


def sum_kernel(finish, n_sum, splits, heads, refs, tail, out_refs, scratch):
    held, done, in_sems, out_sems = scratch
    width = refs[0].shape[1]
    fetches, first_row = [], 0
    for part, rows in enumerate(splits):
        span_from = pl.ds(first_row, rows)
        fetches.append(
            [
                pltpu.make_async_copy(ref.at[span_from, :], held.at[i, span_from, :], in_sems.at[part, i])
                for i, ref in enumerate(refs)
            ]
        )
        for fetch in fetches[-1]:
            fetch.start()
        first_row += rows
    leaves, first_row = [], 0
    for part, rows in enumerate(splits):
        for fetch in fetches[part]:
            fetch.wait()

        @pl.loop(0, rows // ROW_STEP)
        def _(step, first_row=first_row):
            at = pl.ds(pl.multiple_of(first_row + step * ROW_STEP, ROW_STEP), ROW_STEP)
            for first in range(0, width, TILE):
                columns = slice(first, first + TILE)
                values = [held[i, at, columns].astype(jnp.float32) for i in range(len(refs))]
                total = values[0]
                for value in values[1:n_sum]:
                    total = total + value
                for i, result in enumerate(finish(total, *values[n_sum:])):
                    if heads:
                        for lane in range(0, TILE, HEAD_DIM):
                            head = (first + lane) // HEAD_DIM
                            done[i, head, at, :] = result[:, lane : lane + HEAD_DIM].astype(done.dtype)
                    else:
                        done[i, at, columns] = result.astype(done.dtype)

        for i in range(done.shape[0]):
            source = done.at[i] if heads else done.at[i, pl.ds(first_row, rows), :]
            leaves.append(
                pltpu.make_async_copy(source, out_refs[i * len(splits) + part], out_sems.at[part, i])
            )
            leaves[-1].start()
        first_row += rows
    for leave in leaves:
        leave.wait()


def dispatch(kernel, counts, *refs):
    n_arrays, n_tail, n_pass, n_after, n_out = counts
    tail = refs[n_arrays : n_arrays + n_tail]
    outs = refs[n_arrays + n_tail + n_pass + n_after :]
    kernel(refs[:n_arrays], tail, outs[:n_out], outs[n_out + n_pass + 1 :])


class Order:
    def __init__(self):
        self.last = None

    def call(self, kernel, arrays, tail, outs, scratch, passing, vmem, weight=0.0):
        after = [] if self.last is None else [self.last]
        operands = list(arrays) + list(tail) + list(passing) + after
        token = jax.ShapeDtypeStruct((8, HEAD_DIM), jnp.float32)
        n_out, n_pass = len(outs), len(passing)
        first_pass = len(arrays) + len(tail)
        shapes = list(outs) + [jax.ShapeDtypeStruct(p.shape, p.dtype) for p in passing] + [token]
        *results, self.last = pl.pallas_call(
            functools.partial(dispatch, kernel, (len(arrays), len(tail), n_pass, len(after), n_out)),
            in_specs=[pl.BlockSpec(memory_space=pltpu.HBM)] * len(operands),
            out_specs=[pl.BlockSpec(memory_space=pltpu.HBM)] * len(shapes),
            scratch_shapes=scratch,
            out_shape=shapes,
            input_output_aliases={first_pass + i: n_out + i for i in range(n_pass)},
            compiler_params=pltpu.CompilerParams(vmem_limit_bytes=vmem),
            cost_estimate=pl.CostEstimate(flops=1, bytes_accessed=1 + int(weight * COST_STEP), transcendentals=0),
        )(*operands)
        return results

    def stacked(self, arrays):
        width = arrays[0].shape[1]
        pieces = [whole(array) for array in arrays]

        def kernel(refs, tail, out_refs, scratch):
            copies = piece_copies(pieces, refs, out_refs[0], scratch[0])
            for copy in copies:
                copy.start()
            for copy in copies:
                copy.wait()

        shape = (sum(array.shape[0] for array in arrays), width)
        return self.call(
            kernel,
            arrays,
            [],
            [jax.ShapeDtypeStruct(shape, jnp.bfloat16)],
            [pltpu.SemaphoreType.DMA((len(arrays),))],
            (),
            SUM_VMEM,
        )[0]

    def tied(self, arrays):
        return self.call(lambda refs, tail, out_refs, scratch: None, [], [], [], [], arrays, SUM_VMEM)

    def times_weight(self, pieces, weight, mask, splits, transposed, passing=(), tile=TILE):
        depth, width = weight.shape
        x_width, out_width = (width, depth) if transposed else (depth, width)
        rows = sum(piece[2] for piece in pieces)
        w_block = (tile, width) if transposed else (depth, tile)
        return self.call(
            functools.partial(weight_kernel, pieces, transposed, tile),
            [piece[0] for piece in pieces],
            [weight, mask],
            [jax.ShapeDtypeStruct((split, out_width), jnp.bfloat16) for split in splits],
            [
                pltpu.VMEM((rows, x_width), jnp.bfloat16),
                pltpu.VMEM((SLOTS,) + w_block, jnp.bfloat16),
                pltpu.VMEM(w_block, jnp.bfloat16),
                pltpu.VMEM((2, rows, tile), jnp.bfloat16),
                pltpu.VMEM(mask.shape, mask.dtype),
                pltpu.SemaphoreType.DMA((SLOTS,)),
                pltpu.SemaphoreType.DMA((len(pieces),)),
                pltpu.SemaphoreType.DMA((2, len(splits))),
                pltpu.SemaphoreType.DMA,
            ],
            passing,
            MATMUL_VMEM,
            7.0 + 0.02 * max(0, rows - 128),
        )

    def weight_grad(self, x_pieces, g_pieces, mask, scale, passing=(), tile=TILE):
        pieces = list(x_pieces) + list(g_pieces)
        depth, width = x_pieces[0][0].shape[1], g_pieces[0][0].shape[1]
        return self.call(
            functools.partial(grad_kernel, x_pieces, g_pieces, scale, tile),
            [piece[0] for piece in pieces],
            [mask],
            [jax.ShapeDtypeStruct((depth, width), jnp.bfloat16)],
            [
                pltpu.VMEM((sum(piece[2] for piece in x_pieces), depth), jnp.bfloat16),
                pltpu.VMEM((sum(piece[2] for piece in x_pieces), tile), jnp.bfloat16),
                pltpu.VMEM((sum(piece[2] for piece in g_pieces), width), jnp.bfloat16),
                pltpu.VMEM((2, tile, width), jnp.bfloat16),
                pltpu.VMEM(mask.shape, mask.dtype),
                pltpu.SemaphoreType.DMA((2,)),
                pltpu.SemaphoreType.DMA((len(pieces),)),
                pltpu.SemaphoreType.DMA((len(x_pieces),)),
                pltpu.SemaphoreType.DMA,
            ],
            passing,
            MATMUL_VMEM,
            15.0,
        )

    def summed(self, finish, arrays, others=(), n_out=1, splits=None, heads=False, passing=()):
        rows, width = arrays[0].shape
        splits = splits or [rows]
        operands = list(arrays) + list(others)
        shapes = [(width // HEAD_DIM, rows, HEAD_DIM)] if heads else [(split, width) for split in splits]
        whole_shape = shapes[0] if heads else (rows, width)
        outs = [jax.ShapeDtypeStruct(shape, jnp.bfloat16) for shape in shapes] * n_out
        return self.call(
            functools.partial(sum_kernel, finish, len(arrays), splits, heads),
            operands,
            [],
            outs,
            [
                pltpu.VMEM((len(operands), rows, width), jnp.bfloat16),
                pltpu.VMEM((n_out,) + whole_shape, jnp.bfloat16),
                pltpu.SemaphoreType.DMA((len(splits), len(operands))),
                pltpu.SemaphoreType.DMA((len(splits), n_out)),
            ],
            passing,
            SUM_VMEM,
        )


class Chain:
    def __init__(self, order, n_row):
        self.order, self.n_row, self.got = order, n_row, []

    def send(self, value):
        hop = len(self.got)
        pairs = [(hop, hop + 1), (self.n_row - 1 - hop, self.n_row - 2 - hop)]
        self.got.append(lax.ppermute(value, "row", pairs))

    def start(self, part):
        self.part = part
        self.send(part)

    def advance(self):
        self.send(self.order.summed(only_sum, [self.part, self.got[-1]])[0])

    def total(self, finish, others, n_out):
        return self.order.summed(finish, [self.part] + self.got, others, n_out)


def whole(array):
    return (array, 0, array.shape[0])


def halving(n_col):
    places = [0]
    bit = n_col // 2
    while bit:
        places = places + [place + bit for place in places]
        bit //= 2
    return places


def body(tokens, up_weight, up_mask, down_weight, down_mask, grad_out):
    n_row, n_col = lax.axis_size("row"), lax.axis_size("col")
    share = tokens.shape[0]
    grad_scale = 1.0 / math.sqrt(share * n_col)
    chips = n_col // 2
    order = Order()

    def swap(value, offset):
        return lax.ppermute(value, "col", [(i, i ^ offset) for i in range(n_col)])

    tok, cot = [whole(tokens)] + [None] * (n_col - 1), [whole(grad_out)] + [None] * (n_col - 1)
    for offset in range(1, min(6, n_col)):
        tok[offset] = whole(swap(tokens, offset))

    def hold_stacked(offset, value):
        tok[offset], cot[offset] = (value, 0, share), (value, share, share)

    offsets = [[2 * chip, 2 * chip + 1] for chip in range(chips)]
    queue = [("a", c) for c in range(chips)] + [("b", c) for c in range(1, chips)] + [("b", 0)]
    chains = {key: Chain(order, n_row) for key in queue}
    parts, hidden, slope, grad_pre = {}, {}, {}, {}
    results, tok_sums = {}, {}

    def shard_of(held, offset):
        return (held[offset // 2], (offset % 2) * share, share)

    def finish(key):
        kind, chunk = key
        if kind == "a":
            hidden[chunk], slope[chunk] = chains[key].total(gelu_and_slope, [], 2)
        else:
            (grad_pre[chunk],) = chains[key].total(lambda total, rise: (total * rise,), [slope[chunk]], 1)

    def partial(kind, chunks):
        source, weight, mask = (tok, up_weight, up_mask) if kind == "a" else (cot, down_weight, down_mask)

        def run(passing=()):
            pieces = [source[offset] for chunk in chunks for offset in offsets[chunk]]
            outs = order.times_weight(pieces, weight, mask, [2 * share] * len(chunks), kind == "b", passing)
            for chunk, out in zip(chunks, outs):
                parts[kind, chunk] = out
            return outs[len(chunks) :]

        return run

    def work_out(chunks):
        def run(passing=()):
            chosen = [offset for offset in halving(n_col) if offset // 2 in chunks]
            half = share * len(chosen) // 2
            pieces = [shard_of(hidden, offset) for offset in chosen]
            keep, give, *passed = order.times_weight(pieces, down_weight, down_mask, [half, half], False, passing)
            results.setdefault("keeps", []).append(keep)
            results.setdefault("gives", []).append(give)
            results["bit"] = 1
            return passed

        return run

    def give_out():
        if results["bit"] == 1:
            results["keep"], results["give"] = order.stacked(results["keeps"]), order.stacked(results["gives"])
        else:
            (results["give"],) = order.tied([results["give"]])
        results["got"] = swap(results["give"], results["bit"])

    def halve_out(passing=()):
        rows = results["keep"].shape[0]
        arrays = [results["keep"], results["got"]]
        if rows == share:
            results["out"], *passed = order.summed(only_sum, arrays, heads=True, passing=passing)
            return passed
        results["keep"], results["give"], *passed = order.summed(
            only_sum, arrays, splits=[rows // 2, rows // 2], passing=passing
        )
        results["bit"] *= 2
        return passed

    def work_down(passing=()):
        results["down"], *passed = order.weight_grad(
            [whole(hidden[c]) for c in range(chips)],
            [cot[offset] for chunk in offsets for offset in chunk],
            down_mask,
            grad_scale,
            passing,
        )
        return passed

    pending = []

    def work_tok(chunks):
        def run(passing=()):
            kept = [offset for chunk in chunks for offset in offsets[chunk] if offset % 2 == 0]
            given = [offset for chunk in chunks for offset in offsets[chunk] if offset % 2]
            pieces = [shard_of(grad_pre, offset) for offset in kept + given]
            splits = [share * len(group) for group in (kept, given) if group]
            outs = order.times_weight(pieces, up_weight, up_mask, splits, True, passing)
            if chunks == [0]:
                tok_sums[0], tok_sums[1] = outs[0], swap(outs[1], 1)
            else:
                pending.append((kept, outs[0], swap(outs[1], 1)))
            return outs[len(splits) :]

        return run

    def pair_sums():
        while pending:
            kept, keep, got = pending.pop(0)
            sums = order.summed(only_sum, [keep, got], splits=[share] * len(kept))
            for offset, value in zip(kept, sums):
                tok_sums[offset] = swap(value, offset)

    last_slot = len(queue) + n_row - 3
    place_of = {key: i for i, key in enumerate(queue)}

    def ready(key):
        return place_of[key] + n_row - 2

    work = {slot: [] for slot in range(last_slot + 1)}
    work[1].append(partial("a", list(range(3, chips))))
    work[2].append(partial("b", list(range(1, chips)) + [0]))
    last_a = ready(("a", chips - 1))
    work[last_a - 1].append(work_out(list(range(chips - 1))))
    work[last_a].append(work_out([chips - 1]))
    work[last_a + 1].append(work_down)
    held = []
    for chunk in range(1, chips):
        held.append(chunk)
        if ready(("b", chunk)) > last_a + 1:
            work[ready(("b", chunk))].append(work_tok(held))
            held = []

    started = 1

    def start_next(step):
        nonlocal started
        key = queue[started] if started < len(queue) else None
        passing = (parts[key],) if key in parts else ()
        passed = step(passing) if step else order.tied(passing) if passing else ()
        if key is not None:
            parts[key] = passed[0] if passing else parts[key]
            chains[key].start(parts[key])
            started += 1

    partial("a", [0])()
    chains[queue[0]].start(parts[queue[0]])
    start_next(partial("a", list(range(1, min(3, chips)))))
    both = order.stacked([tokens, grad_out])
    late_cot = order.stacked([grad_out])
    near = [(offset, swap(late_cot, offset)) for offset in range(2, min(6, n_col), 2)]
    for slot in range(last_slot + 1):
        for hop in range(n_row - 1):
            at = slot - hop
            if 0 <= at < len(queue):
                if hop < n_row - 2:
                    chains[queue[at]].advance()
                else:
                    finish(queue[at])
        if slot == 0:
            values = order.tied([value for _, value in near])
            for (offset, _), value in zip(near, values):
                cot[offset], cot[offset + 1] = whole(value), whole(swap(value, 1))
            (both,) = order.tied([both])
            far = [(offset, swap(both, offset)) for offset in range(6, n_col, 2)]
        if slot == 1:
            values = order.tied([value for _, value in far] + [late_cot])
            for (offset, _), value in zip(far, values):
                hold_stacked(offset, value)
                hold_stacked(offset + 1, swap(value, 1))
            cot[1] = whole(swap(values[-1], 1))
        pair_sums()
        steps = list(work[slot])
        if slot > last_a and "out" not in results:
            give_out()
            steps.append(halve_out)
        for step in steps[:-1]:
            step()
        start_next(steps[-1] if steps else None)

    work_tok([0])()
    while "out" not in results:
        give_out()
        halve_out()
    (up,) = order.weight_grad(
        [tok[offset] for chunk in offsets for offset in chunk],
        [whole(grad_pre[c]) for c in range(chips)],
        up_mask,
        grad_scale,
    )
    (grad_tokens,) = order.summed(only_sum, [tok_sums[offset] for offset in sorted(tok_sums)])
    return (results["out"], grad_tokens, up, results["down"])


def solution(mesh):
    return jax.shard_map(
        body,
        mesh=mesh,
        in_specs=(
            P("col", "row"),
            P("row", "col"),
            P("row", "col"),
            P("col", "row"),
            P("col", "row"),
            P("col", "row"),
        ),
        out_specs=(P("row", "col", None), P("col", "row"), P("row", "col"), P("col", "row")),
        check_vma=False,
    )
```
